512 devices in a mesh: band: 64 (over z, y), lev: 8 (over x, core).
Axes of the slice: x: 4, y: 8, z: 8, core: 2. Of those that a mesh axis runs over, the one named last changes fastest.
Arguments:
- fourier: bfloat16 [24, 4, 2560, 256], P('lev', None, 'band'), may hold values from -6 to 6
- cycle_points: int32 [2560], P('band'), may hold values from 16 to 5144, as said below
- lat_weight: float32 [2560], P('band'), may hold values from 0.3 to 3
- wave_m: int32 [256], replicated, may hold values from 0 to 1279, as said below
- legendre: bfloat16 [256, 1280, 2560], P('band', 'lev'), may hold values from -0.125 to 0.125
- diffusion: float32 [24], replicated, may hold values from 0.5 to 8
- mode_forward: bfloat16 [24, 24], replicated, may hold values from -1.25 to 1.25
- mode_back: bfloat16 [24, 24], replicated, may hold values from -1.25 to 1.25
- mode_depth: float32 [24], replicated, may hold values from 0.2 to 5
Outputs:
- fourier_new: bfloat16 [24, 4, 2560, 256], P('lev', None, 'band')
The draws below stay inside these ranges and needn't reach their ends.
Inputs may be any that keep to these rules, and one draw needn't show every extreme that they name: `wave_m`: distinct zonal wavenumbers; slot s belongs to the band device of index s // 4; both 0 and 1279 occur. `cycle_points`: a multiple of 4; 16 on the two polar cycles.
All inputs are finite; a program needn't handle non-finite values.
Results may differ from the reference program's by a relative error of at most 0.0062.
Values may be sent and summed in bfloat16 or wider, within the bound.
A program may use at most 128 MiB of HBM per device.

```python
import math
import jax
import jax.numpy as jnp
from jax import lax

NSPEC = 1280
LEVELS = 24
NLAT = 2560
MWAVE = 256


def draw_cycle_points(key, part):
    key = jax.random.fold_in(key, 7)
    cycles = jnp.arange(NLAT, dtype=jnp.int32)
    polar = jnp.minimum(cycles, NLAT - 1 - cycles)
    spacing = max(1, 2560 // NLAT)
    middle = (NLAT - 1) // 2
    jitter = jax.random.randint(key, (NLAT,), 0, 4, dtype=jnp.int32)
    jitter = jnp.where(polar == middle, 3, jitter) * (polar > 0).astype(jnp.int32)
    return (16 + 4 * spacing * polar + 4 * jitter).astype(jnp.int32)


def draw_wave_m(key, part):
    key = jax.random.fold_in(key, 11)
    inner = jax.random.permutation(jax.random.fold_in(key, 1), jnp.arange(1, NSPEC - 1, dtype=jnp.int32))
    chosen = jnp.concatenate([jnp.array([0, NSPEC - 1], dtype=jnp.int32), inner[:MWAVE - 2]])
    return jax.random.permutation(jax.random.fold_in(key, 2), chosen).astype(jnp.int32)


def levels(stream_key, shape, pieces, low, largest):
    def one(position, blocks):
        draws = jax.random.uniform(jax.random.fold_in(jax.random.fold_in(stream_key, 6), position), (blocks,), jnp.float32, low / len(pieces), largest / len(pieces))
        return jnp.repeat(jnp.exp(draws), shape[position] // blocks).reshape((-1,) + (1,) * (len(shape) - position - 1))

    factor_of = one(*pieces[0])
    for cut in pieces[1:]:
        factor_of = factor_of * one(*cut)
    return factor_of


def normal_values(key, extent, scale, reach, cuts=(), kind=jnp.bfloat16):
    drawn = scale * jax.random.normal(key, extent, jnp.float32)
    if cuts:
        drawn = drawn * levels(key, extent, cuts, -0.22, 0.18)
    return jnp.clip(drawn, -reach, reach).astype(kind)


def setup_inputs(seed: int = 0) -> dict:
    streams_of = jax.random.split(jax.random.key(seed), 10)
    return {
        "fourier": normal_values(streams_of[0], (LEVELS, 4, NLAT, MWAVE), 1.0, 6.0, ((0, 8), (2, 64))),
        "cycle_points": draw_cycle_points(jax.random.fold_in(streams_of[9], 71), 0),
        "lat_weight": jnp.clip(jnp.exp(math.log(3.0) - 2.3025851 * jax.random.uniform(streams_of[2], (NLAT,), jnp.float32) ** levels(streams_of[2], (NLAT,), ((0, 64),), -0.2, 0.2)), 0.3, 3.0),
        "wave_m": draw_wave_m(jax.random.fold_in(streams_of[9], 71), 0),
        "legendre": normal_values(streams_of[4], (MWAVE, NSPEC, NLAT), NLAT ** -0.5, 0.125, ((0, 64), (1, 8))),
        "diffusion": jnp.clip(jnp.exp(jax.random.uniform(streams_of[5], (LEVELS,), jnp.float32, math.log(0.5), math.log(8.0))), 0.5, 8.0),
        "mode_forward": normal_values(streams_of[6], (LEVELS, LEVELS), LEVELS ** -0.5, 1.25),
        "mode_back": normal_values(streams_of[7], (LEVELS, LEVELS), LEVELS ** -0.5, 1.25),
        "mode_depth": jnp.clip(jnp.exp(jax.random.uniform(streams_of[8], (LEVELS,), jnp.float32, math.log(0.2), math.log(5.0))), 0.2, 5.0),
    }


def direct_slot(operands):
    matrix, fields, usable = operands
    flat = fields.reshape(-1, fields.shape[-1]).astype(jnp.float32)
    summed = jnp.dot(flat, matrix.astype(jnp.float32).T, precision=lax.Precision.HIGHEST)
    summed = summed.reshape(fields.shape[0], fields.shape[1], -1) * usable[None, None, :]
    return summed.astype(jnp.bfloat16)


def inverse_slot(operands):
    matrix, fields = operands
    flat = fields.reshape(-1, fields.shape[-1]).astype(jnp.float32)
    summed = jnp.dot(flat, matrix.astype(jnp.float32), precision=lax.Precision.HIGHEST)
    return summed.reshape(fields.shape[0], fields.shape[1], -1).astype(jnp.bfloat16)


def reference(fourier, cycle_points, lat_weight, wave_m, legendre, diffusion, mode_forward, mode_back, mode_depth):
    present = (wave_m[:, None] < (cycle_points // 2)[None, :]).astype(jnp.float32)
    present_cycles = present.T
    weighted = (fourier.astype(jnp.float32) * lat_weight[None, None, :, None] * present_cycles[None, None]).astype(jnp.bfloat16)
    columns = jnp.arange(NSPEC, dtype=jnp.int32)
    degree = wave_m[:, None] + columns[None, :]
    usable = (degree <= NSPEC - 1).astype(jnp.float32)
    degree_float = degree.astype(jnp.float32)
    degree_ratio = degree_float * (degree_float + 1.0) / float(NSPEC * (NSPEC - 1))
    per_slot = jnp.transpose(weighted, (3, 0, 1, 2))
    spectral = lax.map(direct_slot, (legendre, per_slot, usable))
    damping = 1.0 + diffusion[None, :, None, None] * (degree_ratio * degree_ratio)[:, None, None, :]
    vorticity = spectral[:, :, 0:2].astype(jnp.float32) / damping
    divergence = spectral[:, :, 2:4].astype(jnp.float32)
    modes = jnp.einsum("kl,slcj->skcj", mode_forward.astype(jnp.float32), divergence, precision=lax.Precision.HIGHEST)
    scaled = (modes / (1.0 + 4.0 * mode_depth[None, :, None, None] * degree_ratio[:, None, None, :])).astype(jnp.bfloat16)
    new_div = jnp.einsum("lk,skcj->slcj", mode_back.astype(jnp.float32), scaled.astype(jnp.float32), precision=lax.Precision.HIGHEST)
    updated = jnp.concatenate([vorticity, new_div], axis=2).astype(jnp.bfloat16)
    gridded = lax.map(inverse_slot, (legendre, updated))
    gridded = jnp.transpose(gridded, (1, 2, 3, 0))
    return gridded * present_cycles[None, None].astype(jnp.bfloat16)
```

```python
import functools
import jax
import jax.numpy as jnp
from jax import lax
from jax.sharding import PartitionSpec as P
from jax.experimental import pallas as pl
from jax.experimental.pallas import tpu as pltpu

F32 = jnp.float32
BF16 = jnp.bfloat16
MESH = pl.DeviceIdType.MESH

LEV3 = 3
COMP = 4
CYC = 40
BANDS = 64
LEVS = 8
CHIPS = 4
GROUP = 16
GROUPS = 4
WIDE = GROUP * CYC
ROWS = 48
DEG = 160
SLOTS = 4
NSPEC = 1280


def iota(shape, dim):
    return lax.broadcasted_iota(jnp.int32, shape, dim)


def column_of(row, count):
    same = iota((count, count), 0) == iota((count, count), 1)
    return jnp.sum(jnp.where(same, row, 0.0), axis=1, keepdims=True)


def kernel(
    four, cyc, latw, wave, leg_hbm, diff, mf, mb, depth, out,
    leg, tmp, send, r1, xall, acc, ut, gf, gb, grecv,
    t1s, t1r, fms, fmr, fps, fpr, esend, r2,
    leg_sem, r1_send, r1_recv, x_send, l_recv, r_recv, far_recv, sib_recv,
    gx_send, gx_recv, t1_send, t1_recv, fm_send, fm_recv, fp_send, fp_recv,
    e_send, r2_recv,
):
    band = lax.axis_index("band")
    lev = lax.axis_index("lev")
    x = lev // 2
    core = lev % 2
    qme = band // GROUP
    right = lax.rem(x + 1, CHIPS) * 2 + core
    left = lax.rem(x + 3, CHIPS) * 2 + core
    far = lax.rem(x + 2, CHIPS) * 2 + core
    sib = x * 2 + 1 - core

    def to_lev(src, dst, s_sem, r_sem, target):
        pltpu.make_async_remote_copy(
            src_ref=src, dst_ref=dst, send_sem=s_sem, recv_sem=r_sem,
            device_id={"lev": target}, device_id_type=MESH,
        ).start()

    def wait_bytes(ref, sem):
        pltpu.make_async_copy(ref, ref, sem).wait()

    barrier = pltpu.get_barrier_semaphore()

    def greet(i, carry):
        pl.semaphore_signal(
            barrier, inc=1, device_id={"band": lax.rem(band + i, BANDS)}, device_id_type=MESH
        )
        return carry

    lax.fori_loop(1, BANDS, greet, 0)
    for other in (right, left, sib):
        pl.semaphore_signal(barrier, inc=1, device_id={"lev": other}, device_id_type=MESH)

    for q in range(GROUPS):
        pltpu.make_async_copy(
            leg_hbm.at[:, pl.ds(q * WIDE, WIDE)], leg.at[q], leg_sem.at[q]
        ).start()

    half = column_of((cyc[...] // 2).astype(F32), CYC)
    weight = column_of(latw[...], CYC)
    waves = wave[...].astype(F32)
    present = waves < half
    scale = jnp.where(present, weight, 0.0)
    for c in range(COMP):
        parts = [four[l, c].astype(F32) * scale for l in range(LEV3)]
        parts.append(jnp.zeros((8, 256), F32))
        tmp[pl.ds(c, 256, stride=4), :] = jnp.concatenate(parts, axis=0).T
    send[...] = tmp[...].reshape(BANDS, 16, 128).astype(BF16)

    pl.semaphore_wait(barrier, BANDS - 1 + 3)

    def scatter(i, carry):
        t = i // GROUP
        turn = t + (t // 2) * (5 - 2 * t)
        there = lax.rem(qme + 4 - turn, GROUPS) * GROUP + lax.rem(band + i, GROUP)

        @pl.when(there != band)
        def _():
            pltpu.make_async_remote_copy(
                src_ref=send.at[there], dst_ref=r1.at[band],
                send_sem=r1_send, recv_sem=r1_recv.at[qme],
                device_id={"band": there}, device_id_type=MESH,
            ).start()

        @pl.when(there == band)
        def _():
            pltpu.make_async_copy(send.at[band], r1.at[band], r1_recv.at[qme]).start()

        return carry

    lax.fori_loop(0, BANDS, scatter, 0)

    cols = LEVS * LEV3 * COMP
    rows = LEVS * ROWS
    levels = LEVS * LEV3
    pick_k = (iota((cols, levels), 0) // COMP == iota((cols, levels), 1)).astype(BF16)
    pick_l = (iota((rows, levels), 0) // 16 == iota((rows, levels), 1)).astype(BF16)
    spread = lax.dot_general(pick_k, mf[...], (((1,), (0,)), ((), ())), preferred_element_type=F32)
    spread = lax.dot_general(
        spread.astype(BF16), pick_l, (((1,), (1,)), ((), ())), preferred_element_type=F32
    )
    row_c = iota((cols, rows), 0) % COMP
    col_c = iota((cols, rows), 1) % COMP
    same_level = iota((cols, rows), 0) // COMP == iota((cols, rows), 1) // 16
    forward = jnp.where(
        row_c == col_c,
        jnp.where(row_c < 2, same_level.astype(F32), spread), 0.0,
    ).astype(BF16)
    back = lax.dot_general(pick_l, mb[...], (((1,), (0,)), ((), ())), preferred_element_type=F32)
    back = lax.dot_general(
        back.astype(BF16), pick_k, (((1,), (1,)), ((), ())), preferred_element_type=F32
    )
    row_b = iota((rows, cols), 0) % COMP
    col_b = iota((rows, cols), 1) % COMP
    same_back = iota((rows, cols), 0) // 16 == iota((rows, cols), 1) // COMP
    backward = jnp.where(
        row_b == col_b,
        jnp.where(row_b < 2, same_back.astype(F32), back), 0.0,
    ).astype(BF16)
    pick_f = iota((cols, levels), 0) // COMP == iota((cols, levels), 1)
    diff_col = jnp.sum(jnp.where(pick_f, diff[...], 0.0), axis=1, keepdims=True)
    depth_col = jnp.sum(jnp.where(pick_f, depth[...], 0.0), axis=1, keepdims=True)
    lane = iota((1, SLOTS * DEG), 1)
    slot_of = lane // DEG
    own = jnp.zeros((1, SLOTS * DEG), F32)
    for s in range(SLOTS):
        mine = iota((1, 256), 1) == band * SLOTS + s
        wave_s = jnp.sum(jnp.where(mine, waves, 0.0), axis=1, keepdims=True)
        own = jnp.where(slot_of == s, wave_s, own)
    degree = own + (lane % DEG + lev * DEG).astype(F32)
    usable = degree <= float(NSPEC - 1)
    ratio = degree * (degree + 1.0) / float(NSPEC * (NSPEC - 1))
    row_col = iota((cols, 1), 0) % COMP
    damping = jnp.where(
        row_col < 2, 1.0 + diff_col * (ratio * ratio), 1.0 + 4.0 * depth_col * ratio
    )

    lane16 = iota((16, 128), 1)

    def turn_of(n):
        t = n + (n // 2) * (5 - 2 * n)
        return lax.rem(qme + t, GROUPS)

    def take(n):
        q = turn_of(n)
        wait_bytes(r1.at[pl.ds(q * GROUP, GROUP)], r1_recv.at[q])
        mine = xall.at[q * LEVS + lev]
        tiles = [r1[q * GROUP + i].astype(F32) for i in range(GROUP)]
        for l in range(LEV3):
            for t in range(WIDE // 128):
                value = None
                for i in range(GROUP):
                    low = CYC * i - 128 * t
                    if low + CYC <= 0 or low >= 128:
                        continue
                    shift = (low - CYC * l) % 128
                    moved = pltpu.roll(tiles[i], shift, 1) if shift else tiles[i]
                    value = moved if value is None else jnp.where(lane16 >= low, moved, value)
                mine[pl.ds(16 * l, 16), pl.ds(128 * t, 128)] = value.astype(BF16)
        to_lev(mine, mine, x_send.at[q], l_recv.at[q], right)
        to_lev(mine, mine, x_send.at[q], r_recv.at[q], left)
        to_lev(mine, mine, x_send.at[q], sib_recv.at[q], sib)

    def relay(n):
        q = turn_of(n)
        from_left = xall.at[q * LEVS + left]
        from_right = xall.at[q * LEVS + right]
        wait_bytes(from_left, l_recv.at[q])
        wait_bytes(from_right, r_recv.at[q])
        onward = q % 2

        @pl.when(onward == 0)
        def _():
            to_lev(from_left, from_left, x_send.at[q], far_recv.at[q], right)

        @pl.when(onward == 1)
        def _():
            to_lev(from_right, from_right, x_send.at[q], far_recv.at[q], left)

        to_lev(from_left, from_left, x_send.at[q], sib_recv.at[q], sib)
        to_lev(from_right, from_right, x_send.at[q], sib_recv.at[q], sib)

    def relay_far(n):
        q = turn_of(n)
        from_far = xall.at[q * LEVS + far]
        wait_bytes(from_far, far_recv.at[q])
        to_lev(from_far, from_far, x_send.at[q], sib_recv.at[q], sib)

    def multiply(n):
        q = turn_of(n)
        wait_bytes(xall.at[pl.ds(0, 4)], sib_recv.at[q])
        wait_bytes(leg.at[q], leg_sem.at[q])
        fields = xall[pl.ds(q * LEVS, LEVS)].reshape(rows, WIDE)
        term = lax.dot_general(
            fields, leg[q], (((1,), (1,)), ((), ())), preferred_element_type=F32
        )

        @pl.when(n == 0)
        def _():
            acc[...] = term

        @pl.when(n > 0)
        def _():
            acc[...] += term

    def direct(n, carry):
        pl.when(n < GROUPS)(lambda: take(n))
        pl.when((n >= 1) & (n < GROUPS + 1))(lambda: relay(n - 1))
        pl.when((n >= 2) & (n < GROUPS + 2))(lambda: relay_far(n - 2))
        pl.when(n >= 3)(lambda: multiply(n - 3))
        return carry

    lax.fori_loop(0, GROUPS + 3, direct, 0)

    own_slot = (iota((rows, 1), 0) // COMP) % SLOTS == slot_of
    spectral = jnp.where(own_slot & usable, acc[...], 0.0).astype(BF16)
    modes = jnp.dot(forward, spectral, preferred_element_type=F32)
    scaled = (modes / damping).astype(BF16)
    updated = jnp.dot(backward, scaled, preferred_element_type=F32)
    ut[...] = jnp.where(own_slot, updated, 0.0).astype(BF16)

    def out_of(n):
        t = (GROUPS - 1) - n
        t = t + (t // 2) * (5 - 2 * t)
        return lax.rem(qme + t, GROUPS)

    def ahead_of(q):
        sense = 1 + 2 * (q % 2)
        ahead = lax.rem(x + sense, CHIPS)
        behind = lax.rem(x + 4 - sense, CHIPS)
        return ahead, behind

    def inverse(n):
        q = out_of(n)
        sums = jnp.dot(ut[...], leg[q], preferred_element_type=F32)
        gf[q] = sums.reshape(LEVS, ROWS, WIDE)
        gb[q] = sums.astype(BF16).reshape(CHIPS, 2, ROWS, WIDE)
        to_lev(gb.at[q, :, 1 - core], grecv.at[q], gx_send.at[q], gx_recv.at[q], sib)

    def chip_sum(q, target):
        return gf[q, target * 2 + core] + grecv[q, target].astype(F32)

    def first_hop(n):
        q = out_of(n)
        wait_bytes(grecv.at[q], gx_recv.at[q])
        ahead, behind = ahead_of(q)
        opposite = lax.rem(x + 2, CHIPS)
        t1s[q] = chip_sum(q, opposite).astype(BF16)
        to_lev(t1s.at[q], t1r.at[q], t1_send.at[q], t1_recv.at[q], ahead * 2 + core)
        fms[q] = chip_sum(q, behind).astype(BF16)
        to_lev(fms.at[q], fmr.at[q], fm_send.at[q], fm_recv.at[q], behind * 2 + core)

    def second_hop(n):
        q = out_of(n)
        ahead, behind = ahead_of(q)
        wait_bytes(t1r.at[q], t1_recv.at[q])
        fps[q] = (chip_sum(q, ahead) + t1r[q].astype(F32)).astype(BF16)
        to_lev(fps.at[q], fpr.at[q], fp_send.at[q], fp_recv.at[q], ahead * 2 + core)

    def give(n):
        q = out_of(n)
        wait_bytes(fmr.at[q], fm_recv.at[q])
        wait_bytes(fpr.at[q], fp_recv.at[q])
        total = chip_sum(q, x) + fmr[q].astype(F32) + fpr[q].astype(F32)
        for i in range(GROUP):
            t, low = divmod(CYC * i, 128)
            value = None
            for l in range(LEV3):
                piece = total[16 * l:16 * l + 16, 128 * t:128 * t + 128]
                shift = (CYC * l - low) % 128
                moved = pltpu.roll(piece, shift, 1) if shift else piece
                if low + CYC > 128:
                    beyond = total[16 * l:16 * l + 16, 128 * t + 128:128 * t + 256]
                    after = pltpu.roll(beyond, shift, 1) if shift else beyond
                    moved = jnp.where(lane16 >= CYC * l + 128 - low, after, moved)
                value = moved if value is None else jnp.where(lane16 >= CYC * l, moved, value)
            esend[q * GROUP + i] = value.astype(BF16)

        def deliver(i, carry):
            there = q * GROUP + lax.rem(band + i, GROUP)

            @pl.when(there != band)
            def _():
                pltpu.make_async_remote_copy(
                    src_ref=esend.at[there], dst_ref=r2.at[band],
                    send_sem=e_send, recv_sem=r2_recv,
                    device_id={"band": there}, device_id_type=MESH,
                ).start()

            @pl.when(there == band)
            def _():
                pltpu.make_async_copy(esend.at[band], r2.at[band], r2_recv).start()

            return carry

        lax.fori_loop(0, GROUP, deliver, 0)

    def back_transform(n, carry):
        pl.when(n < GROUPS)(lambda: inverse(n))
        pl.when((n >= 1) & (n < GROUPS + 1))(lambda: first_hop(n - 1))
        pl.when((n >= 2) & (n < GROUPS + 2))(lambda: second_hop(n - 2))
        pl.when(n >= 3)(lambda: give(n - 3))
        return carry

    lax.fori_loop(0, GROUPS + 3, back_transform, 0)

    wait_bytes(r2, r2_recv)
    tmp[...] = r2[...].astype(F32).reshape(BANDS * 16, 128)
    for c in range(COMP):
        turned = tmp[pl.ds(c, 256, stride=4), :].T
        for l in range(LEV3):
            out[l, c] = jnp.where(present, turned[CYC * l:CYC * l + CYC], 0.0).astype(BF16)

    wait_bytes(send.at[pl.ds(0, BANDS - 1)], r1_send)
    wait_bytes(esend.at[pl.ds(0, BANDS - 1)], e_send)
    for q in range(GROUPS):
        wait_bytes(xall.at[pl.ds(0, 7)], x_send.at[q])
        wait_bytes(grecv.at[q], gx_send.at[q])
        wait_bytes(t1s.at[q], t1_send.at[q])
        wait_bytes(fms.at[q], fm_send.at[q])
        wait_bytes(fps.at[q], fp_send.at[q])


def on_device(
    fourier, cycle_points, lat_weight, wave_m, legendre, diffusion, mode_forward, mode_back,
    mode_depth,
):
    vmem = pl.BlockSpec(memory_space=pltpu.VMEM)
    piece = (GROUPS, ROWS, WIDE)
    dma = pltpu.SemaphoreType.DMA
    return pl.pallas_call(
        kernel,
        out_shape=jax.ShapeDtypeStruct(fourier.shape, BF16),
        in_specs=[vmem] * 4 + [pl.BlockSpec(memory_space=pl.ANY)] + [vmem] * 4,
        out_specs=vmem,
        scratch_shapes=[
            pltpu.VMEM((GROUPS, SLOTS * DEG, WIDE), BF16),
            pltpu.VMEM((BANDS * 16, 128), F32),
            pltpu.VMEM((BANDS, 16, 128), BF16),
            pltpu.VMEM((BANDS, 16, 128), BF16),
            pltpu.VMEM((GROUPS * LEVS, ROWS, WIDE), BF16),
            pltpu.VMEM((LEVS * ROWS, SLOTS * DEG), F32),
            pltpu.VMEM((LEVS * ROWS, SLOTS * DEG), BF16),
            pltpu.VMEM((GROUPS, LEVS, ROWS, WIDE), F32),
            pltpu.VMEM((GROUPS, CHIPS, 2, ROWS, WIDE), BF16),
            pltpu.VMEM((GROUPS, CHIPS, ROWS, WIDE), BF16),
            pltpu.VMEM(piece, BF16),
            pltpu.VMEM(piece, BF16),
            pltpu.VMEM(piece, BF16),
            pltpu.VMEM(piece, BF16),
            pltpu.VMEM(piece, BF16),
            pltpu.VMEM(piece, BF16),
            pltpu.VMEM((BANDS, 16, 128), BF16),
            pltpu.VMEM((BANDS, 16, 128), BF16),
            dma((GROUPS,)),
            dma, dma((GROUPS,)),
            dma((GROUPS,)), dma((GROUPS,)), dma((GROUPS,)), dma((GROUPS,)), dma((GROUPS,)),
            dma((GROUPS,)), dma((GROUPS,)),
            dma((GROUPS,)), dma((GROUPS,)),
            dma((GROUPS,)), dma((GROUPS,)),
            dma((GROUPS,)), dma((GROUPS,)),
            dma, dma,
        ],
        compiler_params=pltpu.CompilerParams(
            collective_id=0, has_side_effects=True, vmem_limit_bytes=40 * 1024 * 1024
        ),
        name="spectral_step",
    )(
        fourier,
        cycle_points.reshape(1, -1),
        lat_weight.reshape(1, -1),
        wave_m.reshape(1, -1),
        legendre.reshape(SLOTS * DEG, GROUPS * WIDE),
        diffusion.reshape(1, -1),
        mode_forward,
        mode_back,
        mode_depth.reshape(1, -1),
    )


def solution(mesh):
    placed = (
        P("lev", None, "band", None),
        P("band"),
        P("band"),
        P(),
        P("band", "lev", None),
        P(),
        P(),
        P(),
        P(),
    )
    return jax.shard_map(
        on_device,
        mesh=mesh,
        in_specs=placed,
        out_specs=P("lev", None, "band", None),
        check_vma=False,
    )
```

```python
import functools
import jax
import jax.numpy as jnp
from jax import lax
from jax.sharding import PartitionSpec as P
from jax.experimental import pallas as pl
from jax.experimental.pallas import tpu as pltpu

F32 = jnp.float32
BF16 = jnp.bfloat16
MESH = pl.DeviceIdType.MESH

LEV3 = 3
COMP = 4
CYC = 40
BANDS = 64
LEVS = 8
CHIPS = 4
GROUP = 16
GROUPS = 4
DIRECT = 3
WIDE = GROUP * CYC
ROWS = 48
DEG = 160
SLOTS = 4
NSPEC = 1280


def iota(shape, dim):
    return lax.broadcasted_iota(jnp.int32, shape, dim)


def column_of(row, count):
    same = iota((count, count), 0) == iota((count, count), 1)
    return jnp.sum(jnp.where(same, row, 0.0), axis=1, keepdims=True)


def kernel(
    four_hbm, cyc_hbm, latw_hbm, wave_hbm, leg_hbm, diff_hbm, mf_hbm, mb_hbm, depth_hbm, out,
    four, cyc, latw, wave, diff, mf, mb, depth, in_sem, leg, tmp, send, r1, xall, acc, ut, gf, gb, grecv,
    t1s, t1r, fms, fmr, fps, fpr, esend, r2,
    leg_sem, r1_send, r1_recv, x_send, l_recv, r_recv, far_recv, sib_recv,
    gx_send, gx_recv, t1_send, t1_recv, fm_send, fm_recv, fp_send, fp_recv,
    e_send, r2_recv,
):
    band = lax.axis_index("band")
    lev = lax.axis_index("lev")
    x = lev // 2
    core = lev % 2
    qme = band // GROUP
    right = lax.rem(x + 1, CHIPS) * 2 + core
    left = lax.rem(x + 3, CHIPS) * 2 + core
    far = lax.rem(x + 2, CHIPS) * 2 + core
    sib = x * 2 + 1 - core

    def to_lev(src, dst, s_sem, r_sem, target):
        pltpu.make_async_remote_copy(
            src_ref=src, dst_ref=dst, send_sem=s_sem, recv_sem=r_sem,
            device_id={"lev": target}, device_id_type=MESH,
        ).start()

    def wait_bytes(ref, sem):
        pltpu.make_async_copy(ref, ref, sem).wait()

    early = [(four_hbm, four), (cyc_hbm, cyc), (latw_hbm, latw), (wave_hbm, wave)]
    late = [(diff_hbm, diff), (mf_hbm, mf), (mb_hbm, mb), (depth_hbm, depth)]
    loads = [
        pltpu.make_async_copy(src, dst, in_sem.at[n]) for n, (src, dst) in enumerate(early + late)
    ]
    for load in loads:
        load.start()

    barrier = pltpu.get_barrier_semaphore()

    for step in (4, 3, 5, 2, 6, 1, 7, 0):
        base = lax.rem(band + 8 * step, BANDS)

        def greet(i, carry):
            other = lax.rem(base + i, BANDS)
            pl.semaphore_signal(
                barrier, inc=1, device_id={"band": other}, device_id_type=MESH
            )
            return carry

        lax.fori_loop(0 if step else 1, 8, greet, 0, unroll=True)
    for other in (far, right, left, sib):
        pl.semaphore_signal(barrier, inc=1, device_id={"lev": other}, device_id_type=MESH)

    for q in range(GROUPS):
        pltpu.make_async_copy(
            leg_hbm.at[:, pl.ds(q * WIDE, WIDE)], leg.at[q], leg_sem.at[q]
        ).start()

    for load in loads[:4]:
        load.wait()
    half = column_of((cyc[...] // 2).astype(F32), CYC)
    weight = column_of(latw[...], CYC)
    waves = wave[...].astype(F32)
    present = waves < half
    scale = jnp.where(present, weight, 0.0)
    for c in range(COMP):
        parts = [four[l, c].astype(F32) * scale for l in range(LEV3)]
        parts.append(jnp.zeros((8, 256), F32))
        tmp[pl.ds(c, 256, stride=4), :] = jnp.concatenate(parts, axis=0).T
    send[...] = tmp[...].reshape(BANDS, 16, 128).astype(BF16)

    pl.semaphore_wait(barrier, BANDS - 1 + 4)

    def scatter(i, carry):
        t = i // GROUP
        turn = t + (t // 2) * (5 - 2 * t)
        there = lax.rem(qme + 4 - turn, GROUPS) * GROUP + lax.rem(band + i, GROUP)

        @pl.when(there != band)
        def _():
            pltpu.make_async_remote_copy(
                src_ref=send.at[there], dst_ref=r1.at[band],
                send_sem=r1_send, recv_sem=r1_recv.at[qme],
                device_id={"band": there}, device_id_type=MESH,
            ).start()

        @pl.when(there == band)
        def _():
            pltpu.make_async_copy(send.at[band], r1.at[band], r1_recv.at[qme]).start()

        return carry

    lax.fori_loop(0, BANDS, scatter, 0)

    for load in loads[4:]:
        load.wait()
    cols = LEVS * LEV3 * COMP
    rows = LEVS * ROWS
    levels = LEVS * LEV3
    pick_k = (iota((cols, levels), 0) // COMP == iota((cols, levels), 1)).astype(BF16)
    pick_l = (iota((rows, levels), 0) // 16 == iota((rows, levels), 1)).astype(BF16)
    spread = lax.dot_general(pick_k, mf[...], (((1,), (0,)), ((), ())), preferred_element_type=F32)
    spread = lax.dot_general(
        spread.astype(BF16), pick_l, (((1,), (1,)), ((), ())), preferred_element_type=F32
    )
    row_c = iota((cols, rows), 0) % COMP
    col_c = iota((cols, rows), 1) % COMP
    same_level = iota((cols, rows), 0) // COMP == iota((cols, rows), 1) // 16
    forward = jnp.where(
        row_c == col_c,
        jnp.where(row_c < 2, same_level.astype(F32), spread), 0.0,
    ).astype(BF16)
    back = lax.dot_general(pick_l, mb[...], (((1,), (0,)), ((), ())), preferred_element_type=F32)
    back = lax.dot_general(
        back.astype(BF16), pick_k, (((1,), (1,)), ((), ())), preferred_element_type=F32
    )
    row_b = iota((rows, cols), 0) % COMP
    col_b = iota((rows, cols), 1) % COMP
    same_back = iota((rows, cols), 0) // 16 == iota((rows, cols), 1) // COMP
    backward = jnp.where(
        row_b == col_b,
        jnp.where(row_b < 2, same_back.astype(F32), back), 0.0,
    ).astype(BF16)
    pick_f = iota((cols, levels), 0) // COMP == iota((cols, levels), 1)
    diff_col = jnp.sum(jnp.where(pick_f, diff[...], 0.0), axis=1, keepdims=True)
    depth_col = jnp.sum(jnp.where(pick_f, depth[...], 0.0), axis=1, keepdims=True)
    lane = iota((1, SLOTS * DEG), 1)
    slot_of = lane // DEG
    own = jnp.zeros((1, SLOTS * DEG), F32)
    for s in range(SLOTS):
        mine = iota((1, 256), 1) == band * SLOTS + s
        wave_s = jnp.sum(jnp.where(mine, waves, 0.0), axis=1, keepdims=True)
        own = jnp.where(slot_of == s, wave_s, own)
    degree = own + (lane % DEG + lev * DEG).astype(F32)
    usable = degree <= float(NSPEC - 1)
    ratio = degree * (degree + 1.0) / float(NSPEC * (NSPEC - 1))
    row_col = iota((cols, 1), 0) % COMP
    damping = jnp.where(
        row_col < 2, 1.0 + diff_col * (ratio * ratio), 1.0 + 4.0 * depth_col * ratio
    )

    lane16 = iota((16, 128), 1)

    def turn_of(n):
        t = n + (n // 2) * (5 - 2 * n)
        return lax.rem(qme + t, GROUPS)

    def take(n):
        q = turn_of(n)
        wait_bytes(r1.at[pl.ds(q * GROUP, GROUP)], r1_recv.at[q])
        mine = xall.at[q * LEVS + lev]
        tiles = [r1[q * GROUP + i].astype(F32) for i in range(GROUP)]
        for l in range(LEV3):
            for t in range(WIDE // 128):
                value = None
                for i in range(GROUP):
                    low = CYC * i - 128 * t
                    if low + CYC <= 0 or low >= 128:
                        continue
                    shift = (low - CYC * l) % 128
                    moved = pltpu.roll(tiles[i], shift, 1) if shift else tiles[i]
                    value = moved if value is None else jnp.where(lane16 >= low, moved, value)
                mine[pl.ds(16 * l, 16), pl.ds(128 * t, 128)] = value.astype(BF16)
        to_lev(mine, mine, x_send.at[q], l_recv.at[q], right)
        to_lev(mine, mine, x_send.at[q], r_recv.at[q], left)
        if n >= DIRECT:
            to_lev(mine, mine, x_send.at[q], far_recv.at[q], far)
        to_lev(mine, mine, x_send.at[q], sib_recv.at[q], sib)

    def relay(n):
        q = turn_of(n)
        from_left = xall.at[q * LEVS + left]
        from_right = xall.at[q * LEVS + right]
        wait_bytes(from_left, l_recv.at[q])
        if n < DIRECT and n % 2 == 0:
            to_lev(from_left, from_left, x_send.at[q], far_recv.at[q], right)
        to_lev(from_left, from_left, x_send.at[q], sib_recv.at[q], sib)
        wait_bytes(from_right, r_recv.at[q])
        if n < DIRECT and n % 2 == 1:
            to_lev(from_right, from_right, x_send.at[q], far_recv.at[q], left)
        to_lev(from_right, from_right, x_send.at[q], sib_recv.at[q], sib)

    def relay_far(n):
        q = turn_of(n)
        from_far = xall.at[q * LEVS + far]
        wait_bytes(from_far, far_recv.at[q])
        to_lev(from_far, from_far, x_send.at[q], sib_recv.at[q], sib)

    def multiply(n):
        q = turn_of(n)
        wait_bytes(xall.at[pl.ds(0, 4)], sib_recv.at[q])
        fields = xall[pl.ds(q * LEVS, LEVS)].reshape(rows, WIDE)
        term = lax.dot_general(
            fields, leg[q], (((1,), (1,)), ((), ())), preferred_element_type=F32
        )
        acc[...] = term if n == 0 else acc[...] + term

    take(0)
    for q in range(GROUPS):
        wait_bytes(leg.at[q], leg_sem.at[q])
    take(1)
    take(2)
    relay(0)
    take(3)
    relay(1)
    relay(2)
    relay_far(0)
    relay(3)
    multiply(0)
    relay_far(1)
    relay_far(3)
    multiply(1)
    relay_far(2)
    multiply(3)
    multiply(2)

    own_slot = (iota((rows, 1), 0) // COMP) % SLOTS == slot_of
    spectral = jnp.where(own_slot & usable, acc[...], 0.0).astype(BF16)
    modes = jnp.dot(forward, spectral, preferred_element_type=F32)
    scaled = (modes / damping).astype(BF16)
    updated = jnp.dot(backward, scaled, preferred_element_type=F32)
    ut[...] = jnp.where(own_slot, updated, 0.0).astype(BF16)

    def out_of(n):
        return lax.rem(qme + (2, 3, 0, 1)[n], GROUPS)

    def ahead_of(n):
        sense = 1 + 2 * (n % 2)
        ahead = lax.rem(x + sense, CHIPS)
        behind = lax.rem(x + 4 - sense, CHIPS)
        return ahead, behind

    def inverse(n):
        q = out_of(n)
        sums = jnp.dot(ut[...], leg[q], preferred_element_type=F32)
        gf[q] = sums.reshape(LEVS, ROWS, WIDE)
        gb[q] = sums.astype(BF16).reshape(CHIPS, 2, ROWS, WIDE)
        to_lev(gb.at[q, :, 1 - core], grecv.at[q], gx_send.at[q], gx_recv.at[q], sib)

    def chip_sum(q, target):
        return gf[q, target * 2 + core] + grecv[q, target].astype(F32)

    def first_hop(n):
        q = out_of(n)
        wait_bytes(grecv.at[q], gx_recv.at[q])
        ahead, behind = ahead_of(n)
        opposite = lax.rem(x + 2, CHIPS)
        t1s[q] = chip_sum(q, opposite).astype(BF16)
        first = far if n >= DIRECT else ahead * 2 + core
        to_lev(t1s.at[q], t1r.at[q], t1_send.at[q], t1_recv.at[q], first)
        fms[q] = chip_sum(q, behind).astype(BF16)
        to_lev(fms.at[q], fmr.at[q], fm_send.at[q], fm_recv.at[q], behind * 2 + core)
        if n >= DIRECT:
            fps[q] = chip_sum(q, ahead).astype(BF16)
            to_lev(fps.at[q], fpr.at[q], fp_send.at[q], fp_recv.at[q], ahead * 2 + core)

    def second_hop(n):
        q = out_of(n)
        ahead, behind = ahead_of(n)
        wait_bytes(t1r.at[q], t1_recv.at[q])
        fps[q] = (chip_sum(q, ahead) + t1r[q].astype(F32)).astype(BF16)
        to_lev(fps.at[q], fpr.at[q], fp_send.at[q], fp_recv.at[q], ahead * 2 + core)

    def give(n):
        q = out_of(n)
        wait_bytes(fmr.at[q], fm_recv.at[q])
        wait_bytes(fpr.at[q], fp_recv.at[q])
        total = chip_sum(q, x) + fmr[q].astype(F32) + fpr[q].astype(F32)
        if n >= DIRECT:
            wait_bytes(t1r.at[q], t1_recv.at[q])
            total = total + t1r[q].astype(F32)
        for i in range(GROUP):
            t, low = divmod(CYC * i, 128)
            value = None
            for l in range(LEV3):
                piece = total[16 * l:16 * l + 16, 128 * t:128 * t + 128]
                shift = (CYC * l - low) % 128
                moved = pltpu.roll(piece, shift, 1) if shift else piece
                if low + CYC > 128:
                    beyond = total[16 * l:16 * l + 16, 128 * t + 128:128 * t + 256]
                    after = pltpu.roll(beyond, shift, 1) if shift else beyond
                    moved = jnp.where(lane16 >= CYC * l + 128 - low, after, moved)
                value = moved if value is None else jnp.where(lane16 >= CYC * l, moved, value)
            esend[q * GROUP + i] = value.astype(BF16)

        def deliver(i, carry):
            there = q * GROUP + lax.rem(band + i, GROUP)

            @pl.when(there != band)
            def _():
                pltpu.make_async_remote_copy(
                    src_ref=esend.at[there], dst_ref=r2.at[band],
                    send_sem=e_send, recv_sem=r2_recv,
                    device_id={"band": there}, device_id_type=MESH,
                ).start()

            @pl.when(there == band)
            def _():
                pltpu.make_async_copy(esend.at[band], r2.at[band], r2_recv).start()

            return carry

        lax.fori_loop(0, GROUP, deliver, 0)

    inverse(0)
    inverse(1)
    inverse(2)
    first_hop(0)
    inverse(3)
    first_hop(1)
    first_hop(2)
    first_hop(3)
    second_hop(0)
    second_hop(1)
    second_hop(2)
    give(0)
    give(3)
    give(1)
    give(2)

    wait_bytes(r2, r2_recv)
    tmp[...] = r2[...].astype(F32).reshape(BANDS * 16, 128)
    for c in range(COMP):
        turned = tmp[pl.ds(c, 256, stride=4), :].T
        for l in range(LEV3):
            out[l, c] = jnp.where(present, turned[CYC * l:CYC * l + CYC], 0.0).astype(BF16)

    wait_bytes(send.at[pl.ds(0, BANDS - 1)], r1_send)
    wait_bytes(esend.at[pl.ds(0, BANDS - 1)], e_send)
    for q in range(GROUPS):
        wait_bytes(xall.at[pl.ds(0, 7)], x_send.at[q])
        wait_bytes(grecv.at[q], gx_send.at[q])
        wait_bytes(t1s.at[q], t1_send.at[q])
        wait_bytes(fms.at[q], fm_send.at[q])
        wait_bytes(fps.at[q], fp_send.at[q])


def on_device(
    fourier, cycle_points, lat_weight, wave_m, legendre, diffusion, mode_forward, mode_back,
    mode_depth,
):
    vmem = pl.BlockSpec(memory_space=pltpu.VMEM)
    piece = (GROUPS, ROWS, WIDE)
    dma = pltpu.SemaphoreType.DMA
    return pl.pallas_call(
        kernel,
        out_shape=jax.ShapeDtypeStruct(fourier.shape, BF16),
        in_specs=[pl.BlockSpec(memory_space=pltpu.HBM)] * 9,
        out_specs=vmem,
        scratch_shapes=[
            pltpu.VMEM((LEV3, COMP, CYC, 256), BF16),
            pltpu.VMEM((1, CYC), jnp.int32),
            pltpu.VMEM((1, CYC), F32),
            pltpu.VMEM((1, 256), jnp.int32),
            pltpu.VMEM((1, LEVS * LEV3), F32),
            pltpu.VMEM((LEVS * LEV3, LEVS * LEV3), BF16),
            pltpu.VMEM((LEVS * LEV3, LEVS * LEV3), BF16),
            pltpu.VMEM((1, LEVS * LEV3), F32),
            dma((8,)),
            pltpu.VMEM((GROUPS, SLOTS * DEG, WIDE), BF16),
            pltpu.VMEM((BANDS * 16, 128), F32),
            pltpu.VMEM((BANDS, 16, 128), BF16),
            pltpu.VMEM((BANDS, 16, 128), BF16),
            pltpu.VMEM((GROUPS * LEVS, ROWS, WIDE), BF16),
            pltpu.VMEM((LEVS * ROWS, SLOTS * DEG), F32),
            pltpu.VMEM((LEVS * ROWS, SLOTS * DEG), BF16),
            pltpu.VMEM((GROUPS, LEVS, ROWS, WIDE), F32),
            pltpu.VMEM((GROUPS, CHIPS, 2, ROWS, WIDE), BF16),
            pltpu.VMEM((GROUPS, CHIPS, ROWS, WIDE), BF16),
            pltpu.VMEM(piece, BF16),
            pltpu.VMEM(piece, BF16),
            pltpu.VMEM(piece, BF16),
            pltpu.VMEM(piece, BF16),
            pltpu.VMEM(piece, BF16),
            pltpu.VMEM(piece, BF16),
            pltpu.VMEM((BANDS, 16, 128), BF16),
            pltpu.VMEM((BANDS, 16, 128), BF16),
            dma((GROUPS,)),
            dma, dma((GROUPS,)),
            dma((GROUPS,)), dma((GROUPS,)), dma((GROUPS,)), dma((GROUPS,)), dma((GROUPS,)),
            dma((GROUPS,)), dma((GROUPS,)),
            dma((GROUPS,)), dma((GROUPS,)),
            dma((GROUPS,)), dma((GROUPS,)),
            dma((GROUPS,)), dma((GROUPS,)),
            dma, dma,
        ],
        compiler_params=pltpu.CompilerParams(
            collective_id=0, has_side_effects=True, vmem_limit_bytes=24 * 1024 * 1024
        ),
        name="spectral_step",
    )(*(pltpu.with_memory_space_constraint(v, pltpu.HBM) for v in (
        fourier,
        cycle_points.reshape(1, -1),
        lat_weight.reshape(1, -1),
        wave_m.reshape(1, -1),
        legendre.reshape(SLOTS * DEG, GROUPS * WIDE),
        diffusion.reshape(1, -1),
        mode_forward,
        mode_back,
        mode_depth.reshape(1, -1),
    )))


def solution(mesh):
    placed = (
        P("lev", None, "band", None),
        P("band"),
        P("band"),
        P(),
        P("band", "lev", None),
        P(),
        P(),
        P(),
        P(),
    )
    return jax.shard_map(
        on_device,
        mesh=mesh,
        in_specs=placed,
        out_specs=P("lev", None, "band", None),
        check_vma=False,
    )
```

```python
import functools
import jax
import jax.numpy as jnp
from jax import lax
from jax.sharding import PartitionSpec as P
from jax.experimental import pallas as pl
from jax.experimental.pallas import tpu as pltpu

F32 = jnp.float32
BF16 = jnp.bfloat16
MESH = pl.DeviceIdType.MESH

LEV3 = 3
COMP = 4
CYC = 40
BANDS = 64
LEVS = 8
CHIPS = 4
GROUP = 16
GROUPS = 4
DIRECT = 3
WIDE = GROUP * CYC
ROWS = 48
DEG = 160
SLOTS = 4
NSPEC = 1280
OUT_TURN = (2, 3, 0, 1)


def iota(shape, dim):
    return lax.broadcasted_iota(jnp.int32, shape, dim)


def column_of(row, count):
    same = iota((count, count), 0) == iota((count, count), 1)
    return jnp.sum(jnp.where(same, row, 0.0), axis=1, keepdims=True)


def kernel(
    four_hbm, cyc_hbm, latw_hbm, wave_hbm, leg_hbm, diff_hbm, mf_hbm, mb_hbm, depth_hbm, out,
    four, cyc, latw, wave, diff, mf, mb, depth, in_sem, leg, tmp, send, r1, xall, acc, ut, gf, gb, grecv,
    t1s, t1r, fms, fmr, fps, fpr, esend, r2,
    leg_sem, r1_send, r1_recv, x_send, l_recv, r_recv, far_recv, sib_recv,
    gx_send, gx_recv, t1_send, t1_recv, fm_send, fm_recv, fp_send, fp_recv,
    e_send, r2_recv,
):
    band = lax.axis_index("band")
    lev = lax.axis_index("lev")
    x = lev // 2
    core = lev % 2
    qme = band // GROUP
    right = lax.rem(x + 1, CHIPS) * 2 + core
    left = lax.rem(x + 3, CHIPS) * 2 + core
    far = lax.rem(x + 2, CHIPS) * 2 + core
    sib = x * 2 + 1 - core

    def to_lev(src, dst, s_sem, r_sem, target):
        pltpu.make_async_remote_copy(
            src_ref=src, dst_ref=dst, send_sem=s_sem, recv_sem=r_sem,
            device_id={"lev": target}, device_id_type=MESH,
        ).start()

    def wait_bytes(ref, sem):
        pltpu.make_async_copy(ref, ref, sem).wait()

    early = [(four_hbm, four), (cyc_hbm, cyc), (latw_hbm, latw), (wave_hbm, wave)]
    late = [(diff_hbm, diff), (mf_hbm, mf), (mb_hbm, mb), (depth_hbm, depth)]
    loads = [
        pltpu.make_async_copy(src, dst, in_sem.at[n]) for n, (src, dst) in enumerate(early + late)
    ]
    for load in loads:
        load.start()

    barrier = pltpu.get_barrier_semaphore()

    for step in (4, 3, 5, 2, 6, 1, 7, 0):
        base = lax.rem(band + 8 * step, BANDS)

        def greet(i, carry):
            other = lax.rem(base + i, BANDS)
            pl.semaphore_signal(
                barrier, inc=1, device_id={"band": other}, device_id_type=MESH
            )
            return carry

        lax.fori_loop(0 if step else 1, 8, greet, 0, unroll=True)
    for other in (far, right, left, sib):
        pl.semaphore_signal(barrier, inc=1, device_id={"lev": other}, device_id_type=MESH)

    for q in range(GROUPS):
        pltpu.make_async_copy(
            leg_hbm.at[:, pl.ds(q * WIDE, WIDE)], leg.at[q], leg_sem.at[q]
        ).start()

    for load in loads[:4]:
        load.wait()
    half = column_of((cyc[...] // 2).astype(F32), CYC)
    weight = column_of(latw[...], CYC)
    waves = wave[...].astype(F32)
    present = waves < half
    scale = jnp.where(present, weight, 0.0)
    for c in range(COMP):
        parts = [four[l, c].astype(F32) * scale for l in range(LEV3)]
        parts.append(jnp.zeros((8, 256), F32))
        tmp[pl.ds(c, 256, stride=4), :] = jnp.concatenate(parts, axis=0).T
    send[...] = tmp[...].reshape(BANDS, 16, 128).astype(BF16)

    pl.semaphore_wait(barrier, BANDS - 1 + 4)

    def send_tiles(turn, src, dst, s_sem, r_sem):
        base = lax.rem(qme + turn, GROUPS) * GROUP

        def one(i, carry):
            there = base + lax.rem(band + i, GROUP)
            pltpu.make_async_remote_copy(
                src_ref=src.at[there], dst_ref=dst.at[band], send_sem=s_sem, recv_sem=r_sem,
                device_id={"band": there}, device_id_type=MESH,
            ).start()
            return carry

        lax.fori_loop(0 if turn else 1, GROUP, one, 0, unroll=True)
        if turn == 0:
            pltpu.make_async_copy(src.at[band], dst.at[band], r_sem).start()

    for turn in (0, 3, 1, 2):
        send_tiles(turn, send, r1, r1_send, r1_recv.at[qme])

    for load in loads[4:]:
        load.wait()
    cols = LEVS * LEV3 * COMP
    rows = LEVS * ROWS
    levels = LEVS * LEV3
    pick_k = (iota((cols, levels), 0) // COMP == iota((cols, levels), 1)).astype(BF16)
    pick_l = (iota((rows, levels), 0) // 16 == iota((rows, levels), 1)).astype(BF16)
    spread = lax.dot_general(pick_k, mf[...], (((1,), (0,)), ((), ())), preferred_element_type=F32)
    spread = lax.dot_general(
        spread.astype(BF16), pick_l, (((1,), (1,)), ((), ())), preferred_element_type=F32
    )
    row_c = iota((cols, rows), 0) % COMP
    col_c = iota((cols, rows), 1) % COMP
    same_level = iota((cols, rows), 0) // COMP == iota((cols, rows), 1) // 16
    forward = jnp.where(
        row_c == col_c,
        jnp.where(row_c < 2, same_level.astype(F32), spread), 0.0,
    ).astype(BF16)
    back = lax.dot_general(pick_l, mb[...], (((1,), (0,)), ((), ())), preferred_element_type=F32)
    back = lax.dot_general(
        back.astype(BF16), pick_k, (((1,), (1,)), ((), ())), preferred_element_type=F32
    )
    row_b = iota((rows, cols), 0) % COMP
    col_b = iota((rows, cols), 1) % COMP
    same_back = iota((rows, cols), 0) // 16 == iota((rows, cols), 1) // COMP
    backward = jnp.where(
        row_b == col_b,
        jnp.where(row_b < 2, same_back.astype(F32), back), 0.0,
    ).astype(BF16)
    pick_f = iota((cols, levels), 0) // COMP == iota((cols, levels), 1)
    diff_col = jnp.sum(jnp.where(pick_f, diff[...], 0.0), axis=1, keepdims=True)
    depth_col = jnp.sum(jnp.where(pick_f, depth[...], 0.0), axis=1, keepdims=True)
    lane = iota((1, SLOTS * DEG), 1)
    slot_of = lane // DEG
    own = jnp.zeros((1, SLOTS * DEG), F32)
    for s in range(SLOTS):
        mine = iota((1, 256), 1) == band * SLOTS + s
        wave_s = jnp.sum(jnp.where(mine, waves, 0.0), axis=1, keepdims=True)
        own = jnp.where(slot_of == s, wave_s, own)
    degree = own + (lane % DEG + lev * DEG).astype(F32)
    usable = degree <= float(NSPEC - 1)
    ratio = degree * (degree + 1.0) / float(NSPEC * (NSPEC - 1))
    row_col = iota((cols, 1), 0) % COMP
    damping = jnp.where(
        row_col < 2, 1.0 + diff_col * (ratio * ratio), 1.0 + 4.0 * depth_col * ratio
    )

    lane16 = iota((16, 128), 1)

    def turn_of(n):
        return lax.rem(qme + (0, 1, 3, 2)[n], GROUPS)

    def take(n):
        q = turn_of(n)
        wait_bytes(r1.at[pl.ds(q * GROUP, GROUP)], r1_recv.at[q])
        mine = xall.at[q * CHIPS + x, core]
        tiles = [r1[q * GROUP + i].astype(F32) for i in range(GROUP)]
        for l in range(LEV3):
            for t in range(WIDE // 128):
                value = None
                for i in range(GROUP):
                    low = CYC * i - 128 * t
                    if low + CYC <= 0 or low >= 128:
                        continue
                    shift = (low - CYC * l) % 128
                    moved = pltpu.roll(tiles[i], shift, 1) if shift else tiles[i]
                    value = moved if value is None else jnp.where(lane16 >= low, moved, value)
                mine[pl.ds(16 * l, 16), pl.ds(128 * t, 128)] = value.astype(BF16)
        for part in range(LEV3):
            level = mine.at[pl.ds(16 * part, 16)]
            to_lev(level, level, x_send.at[q], l_recv.at[q, part], right)
            to_lev(level, level, x_send.at[q], r_recv.at[q, part], left)
        if n >= DIRECT:
            to_lev(mine, mine, x_send.at[q], far_recv.at[q], far)
        to_lev(mine, mine, x_send.at[q], sib_recv.at[q], sib)

    def relay(n):
        q = turn_of(n)
        from_left = xall.at[q * CHIPS + lax.rem(x + 3, CHIPS), core]
        from_right = xall.at[q * CHIPS + lax.rem(x + 1, CHIPS), core]
        for part in range(LEV3):
            level = from_left.at[pl.ds(16 * part, 16)]
            wait_bytes(level, l_recv.at[q, part])
            if n < DIRECT and n % 2 == 0:
                to_lev(level, level, x_send.at[q], far_recv.at[q], right)
        to_lev(from_left, from_left, x_send.at[q], sib_recv.at[q], sib)
        for part in range(LEV3):
            level = from_right.at[pl.ds(16 * part, 16)]
            wait_bytes(level, r_recv.at[q, part])
            if n < DIRECT and n % 2 == 1:
                to_lev(level, level, x_send.at[q], far_recv.at[q], left)
        to_lev(from_right, from_right, x_send.at[q], sib_recv.at[q], sib)

    def relay_far(n):
        q = turn_of(n)
        from_far = xall.at[q * CHIPS + lax.rem(x + 2, CHIPS), core]
        wait_bytes(from_far, far_recv.at[q])
        to_lev(from_far, from_far, x_send.at[q], sib_recv.at[q], sib)

    def term_of(fields, q):
        return lax.dot_general(
            fields.reshape(-1, WIDE), leg[q], (((1,), (1,)), ((), ())),
            preferred_element_type=F32,
        )

    def multiply(n):
        q = turn_of(n)
        wait_bytes(xall.at[pl.ds(0, 2)], sib_recv.at[q])
        term = term_of(xall[pl.ds(q * CHIPS, CHIPS)], q).reshape(acc.shape)
        acc[...] = term if n == 0 else acc[...] + term

    def multiply_plane(n, plane):
        q = turn_of(n)
        term = term_of(xall[pl.ds(q * CHIPS, CHIPS), plane], q)
        acc[:, plane] += term.reshape(CHIPS, ROWS, SLOTS * DEG)

    def multiply_last(n):
        multiply_plane(n, core)
        wait_bytes(xall.at[pl.ds(0, 2)], sib_recv.at[turn_of(n)])
        multiply_plane(n, 1 - core)

    take(0)
    for q in range(GROUPS):
        wait_bytes(leg.at[q], leg_sem.at[q])
    take(1)
    take(2)
    relay(0)
    take(3)
    relay(1)
    relay(2)
    relay_far(0)
    relay(3)
    multiply(0)
    relay_far(1)
    relay_far(3)
    multiply(1)
    relay_far(2)
    multiply(3)
    multiply_last(2)

    own_slot = (iota((rows, 1), 0) // COMP) % SLOTS == slot_of
    spectral = jnp.where(own_slot & usable, acc[...].reshape(rows, SLOTS * DEG), 0.0).astype(BF16)
    modes = jnp.dot(forward, spectral, preferred_element_type=F32)
    scaled = (modes / damping).astype(BF16)
    updated = jnp.dot(backward, scaled, preferred_element_type=F32)
    ut[...] = jnp.where(own_slot, updated, 0.0).astype(BF16).reshape(ut.shape)

    def out_of(n):
        return lax.rem(qme + OUT_TURN[n], GROUPS)

    def ahead_of(n):
        sense = 1 + 2 * (n % 2)
        ahead = lax.rem(x + sense, CHIPS)
        behind = lax.rem(x + 4 - sense, CHIPS)
        return ahead, behind

    def inverse(n):
        q = out_of(n)
        if n == 0:
            theirs = jnp.dot(
                ut[:, 1 - core].reshape(-1, SLOTS * DEG), leg[q], preferred_element_type=F32
            )
            gb[q, :, 1 - core] = theirs.astype(BF16).reshape(CHIPS, ROWS, WIDE)
        else:
            sums = jnp.dot(
                ut[...].reshape(rows, SLOTS * DEG), leg[q], preferred_element_type=F32
            )
            gf[q] = sums.reshape(CHIPS, 2, ROWS, WIDE)
            gb[q] = sums.astype(BF16).reshape(CHIPS, 2, ROWS, WIDE)
        to_lev(gb.at[q, :, 1 - core], grecv.at[q], gx_send.at[q], gx_recv.at[q], sib)
        if n == 0:
            mine = jnp.dot(
                ut[:, core].reshape(-1, SLOTS * DEG), leg[q], preferred_element_type=F32
            )
            gf[q, :, core] = mine.reshape(CHIPS, ROWS, WIDE)

    def chip_sum(q, target):
        return gf[q, target, core] + grecv[q, target].astype(F32)

    def first_hop(n):
        q = out_of(n)
        wait_bytes(grecv.at[q], gx_recv.at[q])
        ahead, behind = ahead_of(n)
        opposite = lax.rem(x + 2, CHIPS)
        t1s[q] = chip_sum(q, opposite).astype(BF16)
        first = far if n >= DIRECT else ahead * 2 + core
        for part in range(LEV3):
            at = pl.ds(16 * part, 16)
            to_lev(t1s.at[q, at], t1r.at[q, at], t1_send.at[q], t1_recv.at[q, part], first)
        fms[q] = chip_sum(q, behind).astype(BF16)
        to_lev(fms.at[q], fmr.at[q], fm_send.at[q], fm_recv.at[q], behind * 2 + core)
        if n >= DIRECT:
            fps[q] = chip_sum(q, ahead).astype(BF16)
            to_lev(fps.at[q], fpr.at[q], fp_send.at[q], fp_recv.at[q], ahead * 2 + core)

    def second_hop(n):
        q = out_of(n)
        ahead, behind = ahead_of(n)
        for part in range(LEV3):
            at = pl.ds(16 * part, 16)
            wait_bytes(t1r.at[q, at], t1_recv.at[q, part])
            mine = gf[q, ahead, core, at] + grecv[q, ahead, at].astype(F32)
            fps[q, at] = (mine + t1r[q, at].astype(F32)).astype(BF16)
            to_lev(
                fps.at[q, at], fpr.at[q, at], fp_send.at[q], fp_recv.at[q], ahead * 2 + core
            )

    def give(n):
        q = out_of(n)
        wait_bytes(fmr.at[q], fm_recv.at[q])
        wait_bytes(fpr.at[q], fp_recv.at[q])
        total = chip_sum(q, x) + fmr[q].astype(F32) + fpr[q].astype(F32)
        if n >= DIRECT:
            for part in range(LEV3):
                wait_bytes(t1r.at[q, pl.ds(16 * part, 16)], t1_recv.at[q, part])
            total = total + t1r[q].astype(F32)
        for i in range(GROUP):
            t, low = divmod(CYC * i, 128)
            value = None
            for l in range(LEV3):
                piece = total[16 * l:16 * l + 16, 128 * t:128 * t + 128]
                shift = (CYC * l - low) % 128
                moved = pltpu.roll(piece, shift, 1) if shift else piece
                if low + CYC > 128:
                    beyond = total[16 * l:16 * l + 16, 128 * t + 128:128 * t + 256]
                    after = pltpu.roll(beyond, shift, 1) if shift else beyond
                    moved = jnp.where(lane16 >= CYC * l + 128 - low, after, moved)
                value = moved if value is None else jnp.where(lane16 >= CYC * l, moved, value)
            esend[q * GROUP + i] = value.astype(BF16)

        send_tiles(OUT_TURN[n], esend, r2, e_send, r2_recv)

    inverse(0)
    inverse(1)
    inverse(2)
    first_hop(0)
    inverse(3)
    first_hop(1)
    first_hop(2)
    first_hop(3)
    second_hop(0)
    second_hop(1)
    second_hop(2)
    give(0)
    give(3)
    give(1)
    give(2)

    wait_bytes(r2, r2_recv)
    tmp[...] = r2[...].astype(F32).reshape(BANDS * 16, 128)
    for c in range(COMP):
        turned = tmp[pl.ds(c, 256, stride=4), :].T
        for l in range(LEV3):
            out[l, c] = jnp.where(present, turned[CYC * l:CYC * l + CYC], 0.0).astype(BF16)

    wait_bytes(send.at[pl.ds(0, BANDS - 1)], r1_send)
    wait_bytes(esend.at[pl.ds(0, BANDS - 1)], e_send)
    for q in range(GROUPS):
        wait_bytes(xall.at[pl.ds(0, 3)], x_send.at[q])
        wait_bytes(xall.at[0, 0], x_send.at[q])
        wait_bytes(grecv.at[q], gx_send.at[q])
        wait_bytes(t1s.at[q], t1_send.at[q])
        wait_bytes(fms.at[q], fm_send.at[q])
        wait_bytes(fps.at[q], fp_send.at[q])


def on_device(
    fourier, cycle_points, lat_weight, wave_m, legendre, diffusion, mode_forward, mode_back,
    mode_depth,
):
    vmem = pl.BlockSpec(memory_space=pltpu.VMEM)
    piece = (GROUPS, ROWS, WIDE)
    dma = pltpu.SemaphoreType.DMA
    return pl.pallas_call(
        kernel,
        out_shape=jax.ShapeDtypeStruct(fourier.shape, BF16),
        in_specs=[pl.BlockSpec(memory_space=pltpu.HBM)] * 9,
        out_specs=vmem,
        scratch_shapes=[
            pltpu.VMEM((LEV3, COMP, CYC, 256), BF16),
            pltpu.VMEM((1, CYC), jnp.int32),
            pltpu.VMEM((1, CYC), F32),
            pltpu.VMEM((1, 256), jnp.int32),
            pltpu.VMEM((1, LEVS * LEV3), F32),
            pltpu.VMEM((LEVS * LEV3, LEVS * LEV3), BF16),
            pltpu.VMEM((LEVS * LEV3, LEVS * LEV3), BF16),
            pltpu.VMEM((1, LEVS * LEV3), F32),
            dma((8,)),
            pltpu.VMEM((GROUPS, SLOTS * DEG, WIDE), BF16),
            pltpu.VMEM((BANDS * 16, 128), F32),
            pltpu.VMEM((BANDS, 16, 128), BF16),
            pltpu.VMEM((BANDS, 16, 128), BF16),
            pltpu.VMEM((GROUPS * CHIPS, 2, ROWS, WIDE), BF16),
            pltpu.VMEM((CHIPS, 2, ROWS, SLOTS * DEG), F32),
            pltpu.VMEM((CHIPS, 2, ROWS, SLOTS * DEG), BF16),
            pltpu.VMEM((GROUPS, CHIPS, 2, ROWS, WIDE), F32),
            pltpu.VMEM((GROUPS, CHIPS, 2, ROWS, WIDE), BF16),
            pltpu.VMEM((GROUPS, CHIPS, ROWS, WIDE), BF16),
            pltpu.VMEM(piece, BF16),
            pltpu.VMEM(piece, BF16),
            pltpu.VMEM(piece, BF16),
            pltpu.VMEM(piece, BF16),
            pltpu.VMEM(piece, BF16),
            pltpu.VMEM(piece, BF16),
            pltpu.VMEM((BANDS, 16, 128), BF16),
            pltpu.VMEM((BANDS, 16, 128), BF16),
            dma((GROUPS,)),
            dma, dma((GROUPS,)),
            dma((GROUPS,)), dma((GROUPS, LEV3)), dma((GROUPS, LEV3)),
            dma((GROUPS,)), dma((GROUPS,)),
            dma((GROUPS,)), dma((GROUPS,)),
            dma((GROUPS,)), dma((GROUPS, LEV3)),
            dma((GROUPS,)), dma((GROUPS,)),
            dma((GROUPS,)), dma((GROUPS,)),
            dma, dma,
        ],
        compiler_params=pltpu.CompilerParams(
            collective_id=0, has_side_effects=True, vmem_limit_bytes=24 * 1024 * 1024
        ),
        name="spectral_step",
    )(*(pltpu.with_memory_space_constraint(v, pltpu.HBM) for v in (
        fourier,
        cycle_points.reshape(1, -1),
        lat_weight.reshape(1, -1),
        wave_m.reshape(1, -1),
        legendre.reshape(SLOTS * DEG, GROUPS * WIDE),
        diffusion.reshape(1, -1),
        mode_forward,
        mode_back,
        mode_depth.reshape(1, -1),
    )))


def solution(mesh):
    placed = (
        P("lev", None, "band", None),
        P("band"),
        P("band"),
        P(),
        P("band", "lev", None),
        P(),
        P(),
        P(),
        P(),
    )
    return jax.shard_map(
        on_device,
        mesh=mesh,
        in_specs=placed,
        out_specs=P("lev", None, "band", None),
        check_vma=False,
    )
```
